512 devices in a mesh: ab: 16 (over x, z_lo), cd: 32 (over y, z_hi, core).
Axes of the slice: x: 4, y: 8, z: 8 (z_hi: 2, z_lo: 4; z = z_hi * 4 + z_lo), core: 2. Of those that a mesh axis runs over, the one named last changes fastest.
Arguments:
- amplitudes: float32 [576, 25600], P('ab', 'cd'), may hold values from -6 to 6
- integrals: float32 [16384, 25600], P('ab', 'cd'), may hold values from -0.0390625 to 0.0390625
- occupied_energy: float32 [24], replicated, may hold values from -2 to -0.4
- virtual_energy: float32 [128], replicated, may hold values from 0.3 to 3
Outputs:
- update: float32 [576, 16384], P('cd', 'ab')
The draws below stay inside these ranges and needn't reach their ends.
All inputs are finite; a program needn't handle non-finite values.
Results may differ from the reference program's by a relative error of at most 0.000071.
Values sent between devices are 32-bit elements; how exact they have to be, the bound alone decides.
A program may use at most 64 MiB of HBM per device.

```python
import jax
import jax.numpy as jnp
from jax import lax

NV = 160
AW = 128
NO = 24


def levels(key, extent, pieces, low, largest):
    def one(position, parts):
        heights = jax.random.uniform(jax.random.fold_in(jax.random.fold_in(key, 6), position), (parts,), jnp.float32, low / len(pieces), largest / len(pieces))
        return jnp.repeat(jnp.exp(heights), extent[position] // parts).reshape((-1,) + (1,) * (len(extent) - position - 1))

    gain = one(*pieces[0])
    for cut in pieces[1:]:
        gain = gain * one(*cut)
    return gain


def normal_values(stream_key, shape, scale, bound, cuts=(), dtype=jnp.bfloat16):
    entries = jax.random.normal(stream_key, shape, jnp.float32) * scale
    if len(cuts) > 0:
        entries = levels(stream_key, shape, cuts, -0.22, 0.18) * entries
    return jnp.clip(entries, min=-bound, max=bound).astype(dtype)


def setup_inputs(seed: int = 0) -> dict:
    splits = jax.random.split(jax.random.key(seed), 5)
    return {
        "amplitudes": normal_values(splits[0], (NO * NO, NV * NV), 1.0, 6.0, ((0, 16), (1, 32)), jnp.float32),
        "integrals": normal_values(splits[1], (AW * AW, NV * NV), (NV * NV) ** -0.5, 0.0390625, ((0, 16), (1, 32)), jnp.float32),
        "occupied_energy": jnp.clip(jax.random.uniform(splits[2], (NO,), jnp.float32, -2.0, -0.4), -2.0, -0.4),
        "virtual_energy": jnp.clip(jax.random.uniform(splits[3], (AW,), jnp.float32, 0.3, 3.0), 0.3, 3.0),
    }


def reference(amplitudes, integrals, occupied_energy, virtual_energy):
    ladder = lax.dot_general(amplitudes, integrals, (((1,), (1,)), ((), ())), precision=lax.Precision.HIGHEST, preferred_element_type=jnp.float32)
    four = ladder.reshape(NO, NO, AW, AW)
    paired = four + jnp.transpose(four, (1, 0, 3, 2))
    occ_pair = occupied_energy[:, None] + occupied_energy[None, :]
    virt_pair = virtual_energy[:, None] + virtual_energy[None, :]
    denominator = virt_pair[None, None, :, :] - occ_pair[:, :, None, None]
    return (paired / denominator).reshape(NO * NO, AW * AW)
```

```python
import functools

import jax
import jax.numpy as jnp
from jax import lax
from jax.experimental import pallas as pl
from jax.experimental.pallas import tpu as pltpu
from jax.sharding import PartitionSpec as P

AW = 128
NO = 24
K = 800
KP = 896
ROWS = 36
OUT_ROWS = 18
PACK = 256
HALF = 128
MESH = pl.DeviceIdType.MESH
F32 = jnp.float32
BF16 = jnp.bfloat16


def remote(src, dst, send, recv, device):
    return pltpu.make_async_remote_copy(
        src_ref=src,
        dst_ref=dst,
        send_sem=send,
        recv_sem=recv,
        device_id=device,
        device_id_type=MESH,
    )


def kernel(
    t_hbm, v_hbm, occ, virt, virt_row, out,
    t_in, v_in, v_cat, t_all, l_f32, lhs, part, core_in, plus_in, minus_in, z_in, total, flip, turned, pieces, done,
    local_sem, z_send, z_recv, xr_send, xr_recv, xl_send, xl_recv, fr_send, fr_recv, fl_send, fl_recv,
    c_send, c_recv, p_send, p_recv, m_send, m_recv, h_send, h_recv, r_send, r_recv, a_send, a_recv,
):
    m, k = lax.axis_index("ab"), lax.axis_index("cd")
    x, z = m // 4, m % 4
    y, zh, c = k // 4, (k // 2) % 2, k % 2
    xl, xr = (x + 3) % 4, (x + 1) % 4
    xf = (x + 2) % 4
    zs = (z, z + 1 - 2 * (z % 2), (z + 2) % 4, 3 - z)
    left, right = (xl * 4 + z, k), (xr * 4 + z, k)
    along_z = [(x * 4 + zs[d], k) for d in range(4)]
    sibling = (m, k + 1 - 2 * c)
    up = (m, ((y + 1) % 8) * 4 + k % 4)
    down = (m, ((y + 7) % 8) * 4 + k % 4)
    across = (m, k + 2 - 4 * zh)

    v_copy = pltpu.make_async_copy(v_hbm, v_in, local_sem.at[0])
    t_copy = pltpu.make_async_copy(t_hbm, t_in, local_sem.at[1])
    t_copy.start()
    v_copy.start()
    barrier = pltpu.get_barrier_semaphore()
    peers = (left, right, *along_z[1:], sibling, up, down, across)
    for peer in peers:
        pl.semaphore_signal(barrier, inc=1, device_id=peer, device_id_type=MESH)

    t_copy.wait()
    for j in range(6):
        t_all[m, pl.ds(ROWS * j, ROWS), :] = t_in[:, 128 * j : 128 * j + 128]
    t_all[m, pl.ds(ROWS * 6, PACK - ROWS * 6), :] = jnp.zeros((PACK - ROWS * 6, 128), F32)
    t_all[m, pl.ds(ROWS * 6, ROWS), 0:32] = t_in[:, 768:800]
    pl.semaphore_wait(barrier, len(peers))

    pending = []

    def go(copy):
        copy.start()
        pending.append(copy)

    def send_x(d):
        block = t_all.at[x * 4 + zs[d]]
        go(remote(block, block, xr_send.at[d], xr_recv.at[d], right))
        go(remote(block, block, xl_send.at[d], xl_recv.at[d], left))

    send_x(0)
    for d in range(1, 4):
        go(remote(t_all.at[m], t_all.at[m], z_send.at[d], z_recv.at[d], along_z[d]))

    v_copy.wait()
    for part_no in range(3):
        v_cat[pl.ds(part_no * KP + K, KP - K), :] = jnp.zeros((KP - K, 1024), BF16)

    def split_v(i, carry):
        rows = pl.ds(pl.multiple_of(i * 80, 80), 80)
        value = v_in[rows, :]
        high = value.astype(BF16)
        low = (value - high.astype(F32)).astype(BF16)
        v_cat[pl.ds(pl.multiple_of(i * 80, 16), 80), :] = high
        v_cat[pl.ds(pl.multiple_of(KP + i * 80, 16), 80), :] = high
        v_cat[pl.ds(pl.multiple_of(2 * KP + i * 80, 16), 80), :] = low
        return carry

    lax.fori_loop(0, K // 80, split_v, 0)
    l_f32[...] = jnp.zeros_like(l_f32)

    def from_z(d):
        block = t_all.at[x * 4 + zs[d]]
        remote(block, block, z_send.at[d], z_recv.at[d], along_z[d]).wait_recv()
        send_x(d)

    def from_x(d):
        block = t_all.at[xl * 4 + zs[d]]
        remote(block, block, xr_send.at[d], xr_recv.at[d], right).wait_recv()
        piece = t_all.at[xl * 4 + zs[d], pl.ds(0, HALF)]
        go(remote(piece, piece, fr_send.at[d], fr_recv.at[d], right))
        block = t_all.at[xr * 4 + zs[d]]
        remote(block, block, xl_send.at[d], xl_recv.at[d], left).wait_recv()
        piece = t_all.at[xr * 4 + zs[d], pl.ds(HALF, HALF)]
        go(remote(piece, piece, fl_send.at[d], fl_recv.at[d], left))

    def group(g):
        for w in range(4):
            slot = g * 4 + w
            for j in range(7):
                l_f32[pl.ds(40 * w, ROWS), 128 * j : 128 * j + 128] = t_all[slot, pl.ds(ROWS * j, ROWS), :]
        value = l_f32[...]
        high = value.astype(BF16)
        lhs[:, 0:KP] = high
        lhs[:, KP : 2 * KP] = (value - high.astype(F32)).astype(BF16)
        lhs[:, 2 * KP : 3 * KP] = high
        for n in range(4):
            product = jnp.dot(lhs[...], v_cat[:, 256 * n : 256 * n + 256], preferred_element_type=F32)
            for w in range(4):
                for h in range(2):
                    part[g * 4 + w, :, 2 * n + h, :] = product[40 * w : 40 * w + ROWS, 128 * h : 128 * h + 128]
        for w in range(4):
            s = g * 4 + w
            go(
                remote(
                    part.at[s, pl.ds(OUT_ROWS * (1 - c), OUT_ROWS)], core_in.at[s],
                    c_send.at[s], c_recv.at[s], sibling,
                )
            )

    from_z(1)
    from_x(0)
    from_z(2)
    from_z(3)
    from_x(1)
    group(x)
    from_x(2)
    from_x(3)
    group(xl)
    group(xr)
    for d in range(4):
        piece = t_all.at[xf * 4 + zs[d], pl.ds(0, HALF)]
        remote(piece, piece, fr_send.at[d], fr_recv.at[d], right).wait_recv()
        piece = t_all.at[xf * 4 + zs[d], pl.ds(HALF, HALF)]
        remote(piece, piece, fl_send.at[d], fl_recv.at[d], left).wait_recv()
    group(xf)

    kind = (1 - zh, zh)

    def own(s):
        mine = pl.ds(OUT_ROWS * c, OUT_ROWS)
        remote(core_in.at[s], core_in.at[s], c_send.at[s], c_recv.at[s], sibling).wait_recv()
        part[s, mine] = part[s, mine] + core_in[s]

    for e in range(2):
        s = ((y + 4) % 8) * 2 + kind[e]
        own(s)
        go(remote(part.at[s, pl.ds(OUT_ROWS * c, 9)], plus_in.at[0, e, pl.ds(0, 9)], p_send.at[0, e], p_recv.at[0, e], up))
        go(remote(part.at[s, pl.ds(OUT_ROWS * c + 9, 9)], minus_in.at[0, e, pl.ds(9, 9)], m_send.at[0, e], m_recv.at[0, e], down))
    for step in range(1, 4):
        for e in range(2):
            for sign in (1, -1):
                into = plus_in if sign == 1 else minus_in
                send, recv, to = (p_send, p_recv, up) if sign == 1 else (m_send, m_recv, down)
                s = ((y + 8 + sign * (4 - step)) % 8) * 2 + kind[e]
                own(s)
                first, count = (0, OUT_ROWS) if step > 1 else (0, 9) if sign == 1 else (9, 9)
                arrived = into.at[step - 1, e, pl.ds(first, count)]
                remote(arrived, arrived, send.at[step - 1, e], recv.at[step - 1, e], to).wait_recv()
                mine = pl.ds(OUT_ROWS * c + first, count)
                part[s, mine] = part[s, mine] + into[step - 1, e, pl.ds(first, count)]
                go(remote(part.at[s, pl.ds(OUT_ROWS * c, OUT_ROWS)], into.at[step, e], send.at[step, e], recv.at[step, e], to))
    for e in range(2):
        s = y * 2 + kind[e]
        own(s)
        remote(plus_in.at[3, e], plus_in.at[3, e], p_send.at[3, e], p_recv.at[3, e], up).wait_recv()
        remote(minus_in.at[3, e], minus_in.at[3, e], m_send.at[3, e], m_recv.at[3, e], down).wait_recv()
        total[e] = part[s, pl.ds(OUT_ROWS * c, OUT_ROWS)] + (plus_in[3, e] + minus_in[3, e])
        if e == 0:
            go(remote(total.at[0], z_in, h_send.at[0], h_recv.at[0], across))
    remote(z_in, z_in, h_send.at[0], h_recv.at[0], across).wait_recv()
    total[1] = total[1] + z_in[...]

    flip[pl.ds(OUT_ROWS, 32 - OUT_ROWS)] = jnp.zeros((32 - OUT_ROWS, 8, 128), F32)

    def mirrored(r):
        row = k * OUT_ROWS + r
        other = (row % NO) * NO + row // NO
        return other // OUT_ROWS, other % OUT_ROWS

    def row_copy(r):
        owner, place = mirrored(r)
        return remote(total.at[1, r], flip.at[place], r_send.at[r], r_recv.at[place], (m, owner))

    def send_row(r, carry):
        owner, place = mirrored(r)

        @pl.when(owner != k)
        def _():
            row_copy(r).start()

        @pl.when(owner == k)
        def _():
            flip[place] = total[1, r]

        return carry

    lax.fori_loop(0, OUT_ROWS, send_row, 0)

    def wait_row(r, carry):
        owner, place = mirrored(r)

        @pl.when(owner != k)
        def _():
            remote(flip.at[r], flip.at[r], r_send.at[r], r_recv.at[r], (m, owner)).wait_recv()

        return carry

    lax.fori_loop(0, OUT_ROWS, wait_row, 0)

    turned[...] = flip[...].reshape(256, 128).T.reshape(16, 8, 256)
    pieces[m] = turned[m]

    def send_piece(d, carry):
        to = (m + d) % 16
        remote(turned.at[to], pieces.at[m], a_send.at[d], a_recv.at[d], (to, k)).start()
        return carry

    lax.fori_loop(1, 16, send_piece, 0)

    lane = lax.broadcasted_iota(jnp.int32, (8, 128), 1)
    sublane = lax.broadcasted_iota(jnp.int32, (8, 128), 0)
    energy = jnp.zeros((8, 128), F32)
    for q in range(8):
        energy = jnp.where(sublane == q, virt[m * 8 + q], energy)
    energy = energy + jnp.broadcast_to(virt_row[...], (8, 128))

    def wait_piece(d, carry):
        source = (m + 16 - d) % 16
        remote(pieces.at[source], pieces.at[source], a_send.at[d], a_recv.at[d], (source, k)).wait_recv()
        return carry

    lax.fori_loop(1, 16, wait_piece, 0)

    low = [pltpu.roll(pieces[q, :, 0:128], 8 * q, 1) if q else pieces[q, :, 0:128] for q in range(16)]
    top = [pltpu.roll(pieces[q, :, 128:256], 8 * q, 1) if q else pieces[q, :, 128:256] for q in range(16)]
    for r in range(OUT_ROWS):
        have = low if r < 16 else top
        shift = r % 16
        mixed = have[0]
        for q in range(1, 16):
            mixed = jnp.where(lane // 8 == (shift + q) % 16, have[q], mixed)
        mirror = pltpu.roll(mixed, 128 - 8 * shift, 1) if shift else mixed
        row = k * OUT_ROWS + r
        below = occ[row // NO] + occ[row % NO]
        done[r] = (total[1, r] + mirror) / (energy - below)
    for q in range(8):
        out[:, 128 * q : 128 * q + 128] = done[:, q, :]

    for copy in pending:
        copy.wait_send()

    def done_row(r, carry):
        owner, place = mirrored(r)

        @pl.when(owner != k)
        def _():
            row_copy(r).wait_send()

        return carry

    lax.fori_loop(0, OUT_ROWS, done_row, 0)

    def done_piece(d, carry):
        to = (m + d) % 16
        remote(turned.at[to], pieces.at[m], a_send.at[d], a_recv.at[d], (to, k)).wait_send()
        return carry

    lax.fori_loop(1, 16, done_piece, 0)


def body(amplitudes, integrals, occupied_energy, virtual_energy):
    dma = pltpu.SemaphoreType.DMA
    call = pl.pallas_call(
        kernel,
        out_shape=jax.ShapeDtypeStruct((OUT_ROWS, 1024), F32),
        in_specs=[
            pl.BlockSpec(memory_space=pltpu.HBM),
            pl.BlockSpec(memory_space=pltpu.HBM),
            pl.BlockSpec(memory_space=pltpu.SMEM),
            pl.BlockSpec(memory_space=pltpu.SMEM),
            pl.BlockSpec(memory_space=pltpu.VMEM),
        ],
        out_specs=pl.BlockSpec(memory_space=pltpu.VMEM),
        scratch_shapes=[
            pltpu.VMEM((ROWS, K), F32),
            pltpu.VMEM((K, 1024), F32),
            pltpu.VMEM((3 * KP, 1024), BF16),
            pltpu.VMEM((16, PACK, 128), F32),
            pltpu.VMEM((160, KP), F32),
            pltpu.VMEM((160, 3 * KP), BF16),
            pltpu.VMEM((16, ROWS, 8, 128), F32),
            pltpu.VMEM((16, OUT_ROWS, 8, 128), F32),
            pltpu.VMEM((4, 2, OUT_ROWS, 8, 128), F32),
            pltpu.VMEM((4, 2, OUT_ROWS, 8, 128), F32),
            pltpu.VMEM((OUT_ROWS, 8, 128), F32),
            pltpu.VMEM((2, OUT_ROWS, 8, 128), F32),
            pltpu.VMEM((32, 8, 128), F32),
            pltpu.VMEM((16, 8, 256), F32),
            pltpu.VMEM((16, 8, 256), F32),
            pltpu.VMEM((OUT_ROWS, 8, 128), F32),
            dma((2,)),
            dma((4,)), dma((4,)),
            dma((4,)), dma((4,)), dma((4,)), dma((4,)),
            dma((4,)), dma((4,)), dma((4,)), dma((4,)),
            dma((16,)), dma((16,)),
            dma((4, 2)), dma((4, 2)), dma((4, 2)), dma((4, 2)),
            dma((1,)), dma((1,)),
            dma((OUT_ROWS,)), dma((OUT_ROWS,)),
            dma((16,)), dma((16,)),
        ],
        compiler_params=pltpu.CompilerParams(
            collective_id=0, has_side_effects=True, vmem_limit_bytes=48 * 1024 * 1024
        ),
    )
    return call(
        amplitudes,
        integrals.T,
        occupied_energy,
        virtual_energy,
        virtual_energy.reshape(1, AW),
    )


def solution(mesh):
    return jax.shard_map(
        body,
        mesh=mesh,
        in_specs=(P("ab", "cd"), P("ab", "cd"), P(), P()),
        out_specs=P("cd", "ab"),
        check_vma=False,
    )
```

```python
import functools

import jax
import jax.numpy as jnp
from jax import lax
from jax.experimental import pallas as pl
from jax.experimental.pallas import tpu as pltpu
from jax.sharding import PartitionSpec as P

AW = 128
NO = 24
K = 800
KP = 896
ROWS = 36
OUT_ROWS = 18
PACK = 232
TAIL = 9
CUTS = ((0, 56), (56, 64), (120, 56), (176, 56))
MESH = pl.DeviceIdType.MESH
F32 = jnp.float32
BF16 = jnp.bfloat16


def remote(src, dst, send, recv, device):
    return pltpu.make_async_remote_copy(
        src_ref=src,
        dst_ref=dst,
        send_sem=send,
        recv_sem=recv,
        device_id=device,
        device_id_type=MESH,
    )


def kernel(
    t_hbm, v_hbm, occ_hbm, virt_hbm, row_hbm, out,
    t_in, v_in, occ, virt, virt_row, v_cat, t_all, l_f32, lhs, part, core_in, plus_in, minus_in, z_in, total, flip,
    turned, pieces, done,
    local_sem, g_send, g_recv,
    c_send, c_recv, p_send, p_recv, m_send, m_recv, h_send, h_recv, r_send, r_recv, a_send, a_recv,
):
    m, k = lax.axis_index("ab"), lax.axis_index("cd")
    x, z = lax.div(m, 4), lax.rem(m, 4)
    y, zh, c = lax.div(k, 4), lax.rem(lax.div(k, 2), 2), lax.rem(k, 2)
    xl, xr, xf = lax.rem(x + 3, 4), lax.rem(x + 1, 4), lax.rem(x + 2, 4)
    zs = (z, z + 1 - 2 * lax.rem(z, 2), lax.rem(z + 2, 4), 3 - z)
    near = lax.div(z, 2)
    left, right = (xl * 4 + z, k), (xr * 4 + z, k)
    along_z = [(x * 4 + zs[d], k) for d in range(4)]
    sibling = (m, k + 1 - 2 * c)
    up = (m, lax.rem(y + 1, 8) * 4 + lax.rem(k, 4))
    down = (m, lax.rem(y + 7, 8) * 4 + lax.rem(k, 4))
    across = (m, k + 2 - 4 * zh)

    t_copy = pltpu.make_async_copy(t_hbm, t_in, local_sem.at[0])
    t_copy.start()
    v_copy = pltpu.make_async_copy(v_hbm, v_in, local_sem.at[1])
    v_copy.start()
    small = [
        pltpu.make_async_copy(occ_hbm, occ, local_sem.at[2]),
        pltpu.make_async_copy(virt_hbm, virt, local_sem.at[3]),
        pltpu.make_async_copy(row_hbm, virt_row, local_sem.at[4]),
    ]
    for copy in small:
        copy.start()
    barrier = pltpu.get_barrier_semaphore()
    peers = (left, right, *along_z[1:], sibling, up, down, across)
    for peer in peers:
        pl.semaphore_signal(barrier, inc=1, device_id=peer, device_id_type=MESH)

    t_copy.wait()
    for j in range(6):
        t_all[m, pl.ds(ROWS * j, ROWS), :] = t_in[:, 128 * j : 128 * j + 128]
    t_all[m, pl.ds(ROWS * 6, TAIL), :] = jnp.concatenate(
        [t_in[TAIL * q : TAIL * q + TAIL, 768:800] for q in range(4)], axis=1
    )
    t_all[m, pl.ds(ROWS * 6 + TAIL, PACK - ROWS * 6 - TAIL), :] = jnp.zeros((PACK - ROWS * 6 - TAIL, 128), F32)
    pl.semaphore_wait(barrier, len(peers))

    pending = []

    def go(copy):
        copy.start()
        pending.append(copy)

    def await_into(ref, send, recv, device):
        remote(ref, ref, send, recv, device).wait_recv()

    xs = (x, xl, xr, xf)
    links = {"right": right, "left": left, "z1": along_z[1], "z2": along_z[2], "z3": along_z[3]}
    sent = {}

    def place_at(way, g, d):
        if way == "right":
            return (1 if g == 0 else 3), d
        if way == "left":
            return (2 if g == 0 else 3), d
        return g, d ^ int(way[1])

    def give(way, g, d, q):
        there, depth = place_at(way, g, d)
        number = sent.setdefault((way, g, d), [len(sent), []])
        number[1].append(q)
        piece = t_all.at[xs[g] * 4 + zs[d], pl.ds(*CUTS[q])]
        remote(piece, piece, g_send.at[number[0]], g_recv.at[there * 4 + depth, q], links[way]).start()

    def take(g, d, q):
        await_into(t_all.at[xs[g] * 4 + zs[d], pl.ds(*CUTS[q])], g_send.at[0], g_recv.at[g * 4 + d, q], right)

    def give_x(d, q):
        give("right", 0, d, q)
        give("left", 0, d, q)

    def from_sides(d, q):
        take(1, d, q)
        if q < 2:
            give("right", 1, d, q)
        take(2, d, q)
        if q >= 2:
            give("left", 2, d, q)

    every = range(4)
    for way in ("right", "left", "z1", "z2", "z3"):
        for q in every:
            give(way, 0, 0, q)

    l_f32[...] = jnp.zeros_like(l_f32)
    for part_no in range(2):
        v_cat[pl.ds(part_no * KP + K, KP - K), :] = jnp.zeros((KP - K, 1024), BF16)
    v_copy.wait()

    def split_v(i, carry):
        value = v_in[pl.ds(pl.multiple_of(i * 80, 80), 80), :]
        high = value.astype(BF16)
        low = (value - high.astype(F32)).astype(BF16)
        v_cat[pl.ds(pl.multiple_of(i * 80, 16), 80), :] = high
        v_cat[pl.ds(pl.multiple_of(KP + i * 80, 16), 80), :] = low
        return carry

    lax.fori_loop(0, K // 80, split_v, 0)
    def multiply(slots):
        many = len(slots)
        for w, slot in enumerate(slots):
            for j in range(6):
                l_f32[pl.ds(40 * w, ROWS), 128 * j : 128 * j + 128] = t_all[slot, pl.ds(ROWS * j, ROWS), :]
            for q in range(4):
                l_f32[pl.ds(40 * w + TAIL * q, TAIL), 768:800] = t_all[slot, pl.ds(ROWS * 6, TAIL), 32 * q : 32 * q + 32]
        size = 40 * many
        value = l_f32[0:size, :]
        high = value.astype(BF16)
        lhs[0:size, :] = high
        lhs[size : 2 * size, :] = (value - high.astype(F32)).astype(BF16)
        for n in range(4):
            both = jnp.dot(lhs[0 : 2 * size, :], v_cat[0:KP, 256 * n : 256 * n + 256], preferred_element_type=F32)
            rest = jnp.dot(lhs[0:size, :], v_cat[KP : 2 * KP, 256 * n : 256 * n + 256], preferred_element_type=F32)
            product = both[0:size] + (both[size : 2 * size] + rest)
            for w, slot in enumerate(slots):
                for h in range(2):
                    part[slot, :, 2 * n + h, :] = product[40 * w : 40 * w + ROWS, 128 * h : 128 * h + 128]
        for slot in slots:
            share = part.at[slot, pl.ds(OUT_ROWS * (1 - c), OUT_ROWS)]
            go(remote(share, core_in.at[slot], c_send.at[slot], c_recv.at[slot], sibling))

    for q in every:
        from_sides(0, q)
        if q >= 2:
            give("z1", 1, 0, q)
            give("z1", 2, 0, q)
    for q in (0, 1):
        take(0, 1, q)
        give_x(1, q)
    for q in every:
        take(0, 2, q)
        give_x(2, q)
    for q in every:
        from_sides(1, q)
    for q in every:
        take(0, 3, q)
        give_x(3, q)
    for q in every:
        from_sides(2, q)
    for q in (2, 3):
        take(0, 1, q)
    multiply([x * 4 + w for w in range(4)])
    for q in every:
        from_sides(3, q)
    multiply([xl * 4 + w for w in range(4)])
    multiply([xr * 4 + w for w in range(4)])
    for d in (0, 1):
        for q in every:
            take(3, d, q)
    multiply([xf * 4 + 2 * near, xf * 4 + 2 * near + 1])
    for d in (2, 3):
        for q in every:
            take(3, d, q)
    multiply([xf * 4 + 2 - 2 * near, xf * 4 + 3 - 2 * near])

    kind = (1 - zh, zh)

    def own(s):
        await_into(core_in.at[s], c_send.at[s], c_recv.at[s], sibling)
        mine = pl.ds(OUT_ROWS * c, OUT_ROWS)
        part[s, mine] = part[s, mine] + core_in[s]

    ways = ((1, plus_in, p_send, p_recv, up), (-1, minus_in, m_send, m_recv, down))
    nine = (pl.ds(0, 9), pl.ds(9, 9))

    def share_of(s, h):
        return part.at[s, pl.ds(OUT_ROWS * c + 9 * h, 9)]

    for e in range(2):
        s = lax.rem(y + 4, 8) * 2 + kind[e]
        own(s)
        for h, (_, into, send, recv, to) in enumerate(ways):
            go(remote(share_of(s, h), into.at[0, e, nine[h]], send.at[0, e, h], recv.at[0, e, h], to))
    for step in range(1, 4):
        for e in range(2):
            owners = [lax.rem(y + 8 + sign * (4 - step), 8) * 2 + kind[e] for sign in (1, -1)]
            for s in owners:
                own(s)
            for h in range(2):
                for turn, (s, (_, into, send, recv, to)) in enumerate(zip(owners, ways)):
                    if step > 1 or h == turn:
                        await_into(into.at[step - 1, e, nine[h]], send.at[step - 1, e, h], recv.at[step - 1, e, h], to)
                        mine = pl.ds(OUT_ROWS * c + 9 * h, 9)
                        part[s, mine] = part[s, mine] + into[step - 1, e, nine[h]]
                    go(remote(share_of(s, h), into.at[step, e, nine[h]], send.at[step, e, h], recv.at[step, e, h], to))
    for e in range(2):
        s = y * 2 + kind[e]
        own(s)
        for h in range(2):
            for _, into, send, recv, to in ways:
                await_into(into.at[3, e, nine[h]], send.at[3, e, h], recv.at[3, e, h], to)
            total[e, nine[h]] = part[s, pl.ds(OUT_ROWS * c + 9 * h, 9)] + (plus_in[3, e, nine[h]] + minus_in[3, e, nine[h]])
            if e == 0:
                go(remote(total.at[0, nine[h]], z_in.at[nine[h]], h_send.at[h], h_recv.at[h], across))

    i0 = lax.div(k * OUT_ROWS, NO)
    j0 = k * OUT_ROWS - i0 * NO

    def indices(r):
        wrap = jnp.where(j0 + r >= NO, 1, 0)
        return i0 + wrap, j0 + r - NO * wrap

    def mirrored(r):
        i, j = indices(r)
        other = j * NO + i
        owner = lax.div(other * 3641, 65536)
        return owner, other - owner * OUT_ROWS

    def row_copy(r, owner, place):
        return remote(total.at[1, r], flip.at[place], r_send.at[r], r_recv.at[place], (m, owner))

    def send_row(r, carry):
        owner, place = mirrored(r)

        @pl.when(owner != k)
        def _():
            row_copy(r, owner, place).start()

        @pl.when(owner == k)
        def _():
            flip[place] = total[1, r]

        return carry

    for h in range(2):
        await_into(z_in.at[nine[h]], h_send.at[h], h_recv.at[h], across)
        total[1, nine[h]] = total[1, nine[h]] + z_in[nine[h]]
        lax.fori_loop(9 * h, 9 * h + 9, send_row, 0)

    flip[pl.ds(OUT_ROWS, 32 - OUT_ROWS)] = jnp.zeros((32 - OUT_ROWS, 8, 128), F32)
    for copy in small:
        copy.wait()
    lane = lax.broadcasted_iota(jnp.int32, (8, 128), 1)
    sublane = lax.broadcasted_iota(jnp.int32, (8, 128), 0)
    energy = jnp.zeros((8, 128), F32)
    for q in range(8):
        energy = jnp.where(sublane == q, virt[m * 8 + q], energy)
    energy = energy + jnp.broadcast_to(virt_row[...], (8, 128))
    for copy in pending:
        copy.wait_send()

    for (way, g, d), (number, pieces_sent) in sent.items():
        first, last = min(pieces_sent), max(pieces_sent)
        start = CUTS[first][0]
        span = t_all.at[xs[g] * 4 + zs[d], pl.ds(start, sum(CUTS[last]) - start)]
        remote(span, span, g_send.at[number], g_recv.at[0, 0], links[way]).wait_send()

    def wait_row(r, carry):
        owner, place = mirrored(r)

        @pl.when(owner != k)
        def _():
            await_into(flip.at[r], r_send.at[r], r_recv.at[r], (m, owner))
            row_copy(r, owner, place).wait_send()

        return carry

    lax.fori_loop(0, OUT_ROWS, wait_row, 0)

    turned[...] = flip[...].reshape(256, 128).T.reshape(16, 8, 256)

    def piece_copy(d):
        to = lax.rem(m + d, 16)
        return remote(turned.at[to], pieces.at[m], a_send.at[d], a_recv.at[d], (to, k))

    def send_piece(d, carry):
        piece_copy(d).start()
        return carry

    lax.fori_loop(1, 16, send_piece, 0)
    pieces[m] = turned[m]

    def wait_piece(d, carry):
        source = lax.rem(m + 16 - d, 16)
        await_into(pieces.at[source], a_send.at[d], a_recv.at[d], (source, k))
        piece_copy(d).wait_send()
        return carry

    lax.fori_loop(1, 16, wait_piece, 0)

    low = [pltpu.roll(pieces[q, :, 0:128], 8 * q, 1) if q else pieces[q, :, 0:128] for q in range(16)]
    top = [pltpu.roll(pieces[q, :, 128:256], 8 * q, 1) if q else pieces[q, :, 128:256] for q in range(16)]
    for r in range(OUT_ROWS):
        have = low if r < 16 else top
        shift = r % 16
        mixed = have[0]
        for q in range(1, 16):
            mixed = jnp.where(lane // 8 == (shift + q) % 16, have[q], mixed)
        mirror = pltpu.roll(mixed, 128 - 8 * shift, 1) if shift else mixed
        i, j = indices(r)
        done[r] = (total[1, r] + mirror) / (energy - (occ[i] + occ[j]))
    for q in range(8):
        out[:, 128 * q : 128 * q + 128] = done[:, q, :]


def body(amplitudes, integrals, occupied_energy, virtual_energy):
    dma = pltpu.SemaphoreType.DMA
    call = pl.pallas_call(
        kernel,
        out_shape=jax.ShapeDtypeStruct((OUT_ROWS, 1024), F32),
        in_specs=[pl.BlockSpec(memory_space=pltpu.HBM)] * 5,
        out_specs=pl.BlockSpec(memory_space=pltpu.VMEM),
        scratch_shapes=[
            pltpu.VMEM((ROWS, K), F32),
            pltpu.VMEM((K, 1024), F32),
            pltpu.SMEM((NO,), F32),
            pltpu.SMEM((AW,), F32),
            pltpu.VMEM((1, AW), F32),
            pltpu.VMEM((2 * KP, 1024), BF16),
            pltpu.VMEM((16, PACK, 128), F32),
            pltpu.VMEM((160, KP), F32),
            pltpu.VMEM((320, KP), BF16),
            pltpu.VMEM((16, ROWS, 8, 128), F32),
            pltpu.VMEM((16, OUT_ROWS, 8, 128), F32),
            pltpu.VMEM((4, 2, OUT_ROWS, 8, 128), F32),
            pltpu.VMEM((4, 2, OUT_ROWS, 8, 128), F32),
            pltpu.VMEM((OUT_ROWS, 8, 128), F32),
            pltpu.VMEM((2, OUT_ROWS, 8, 128), F32),
            pltpu.VMEM((32, 8, 128), F32),
            pltpu.VMEM((16, 8, 256), F32),
            pltpu.VMEM((16, 8, 256), F32),
            pltpu.VMEM((OUT_ROWS, 8, 128), F32),
            dma((5,)),
            dma((21,)), dma((16, 4)),
            dma((16,)), dma((16,)),
            dma((4, 2, 2)), dma((4, 2, 2)), dma((4, 2, 2)), dma((4, 2, 2)),
            dma((2,)), dma((2,)),
            dma((OUT_ROWS,)), dma((OUT_ROWS,)),
            dma((16,)), dma((16,)),
        ],
        compiler_params=pltpu.CompilerParams(
            collective_id=0, has_side_effects=True, vmem_limit_bytes=48 * 1024 * 1024
        ),
    )
    return call(
        *(
            pltpu.with_memory_space_constraint(value, pltpu.HBM)
            for value in (
                amplitudes,
                integrals.T,
                occupied_energy,
                virtual_energy,
                virtual_energy.reshape(1, AW),
            )
        )
    )


def solution(mesh):
    return jax.shard_map(
        body,
        mesh=mesh,
        in_specs=(P("ab", "cd"), P("ab", "cd"), P(), P()),
        out_specs=P("cd", "ab"),
        check_vma=False,
    )
```

```python
import functools

import jax
import jax.numpy as jnp
from jax import lax
from jax.experimental import pallas as pl
from jax.experimental.pallas import tpu as pltpu
from jax.sharding import PartitionSpec as P

AW = 128
NO = 24
K = 800
KP = 896
ROWS = 36
OUT_ROWS = 18
PACK = 232
TAIL = 9
CUTS = ((0, 56), (56, 64), (120, 56), (176, 56))
MESH = pl.DeviceIdType.MESH
F32 = jnp.float32
BF16 = jnp.bfloat16


def remote(src, dst, send, recv, device):
    return pltpu.make_async_remote_copy(
        src_ref=src,
        dst_ref=dst,
        send_sem=send,
        recv_sem=recv,
        device_id=device,
        device_id_type=MESH,
    )


def kernel(
    t_hbm, v_hbm, occ_hbm, virt_hbm, row_hbm, out,
    t_in, v_in, occ, virt, virt_row, v_cat, t_all, l_f32, lhs, part, core_in, plus_in, minus_in, z_in, total, flip,
    turned, pieces, done,
    local_sem, g_send, g_recv,
    c_send, c_recv, p_send, p_recv, m_send, m_recv, h_send, h_recv, r_send, r_recv, a_send, a_recv,
):
    m, k = lax.axis_index("ab"), lax.axis_index("cd")
    x, z = lax.div(m, 4), lax.rem(m, 4)
    y, zh, c = lax.div(k, 4), lax.rem(lax.div(k, 2), 2), lax.rem(k, 2)
    xl, xr, xf = lax.rem(x + 3, 4), lax.rem(x + 1, 4), lax.rem(x + 2, 4)
    zs = (z, z + 1 - 2 * lax.rem(z, 2), lax.rem(z + 2, 4), 3 - z)
    near = lax.div(z, 2)
    left, right = (xl * 4 + z, k), (xr * 4 + z, k)
    along_z = [(x * 4 + zs[d], k) for d in range(4)]
    sibling = (m, k + 1 - 2 * c)
    up = (m, lax.rem(y + 1, 8) * 4 + lax.rem(k, 4))
    down = (m, lax.rem(y + 7, 8) * 4 + lax.rem(k, 4))
    across = (m, k + 2 - 4 * zh)

    t_copy = pltpu.make_async_copy(t_hbm, t_in, local_sem.at[0])
    t_copy.start()
    v_copy = pltpu.make_async_copy(v_hbm, v_in, local_sem.at[1])
    v_copy.start()
    small = [
        pltpu.make_async_copy(occ_hbm, occ, local_sem.at[2]),
        pltpu.make_async_copy(virt_hbm, virt, local_sem.at[3]),
        pltpu.make_async_copy(row_hbm, virt_row, local_sem.at[4]),
    ]
    for copy in small:
        copy.start()
    barrier = pltpu.get_barrier_semaphore()
    peers = (left, right, *along_z[1:], sibling, up, down, across)
    for peer in peers:
        pl.semaphore_signal(barrier, inc=1, device_id=peer, device_id_type=MESH)

    t_copy.wait()
    for j in range(6):
        t_all[m, pl.ds(ROWS * j, ROWS), :] = t_in[:, 128 * j : 128 * j + 128]
    t_all[m, pl.ds(ROWS * 6, TAIL), :] = jnp.concatenate(
        [t_in[TAIL * q : TAIL * q + TAIL, 768:800] for q in range(4)], axis=1
    )
    t_all[m, pl.ds(ROWS * 6 + TAIL, PACK - ROWS * 6 - TAIL), :] = jnp.zeros((PACK - ROWS * 6 - TAIL, 128), F32)
    pl.semaphore_wait(barrier, len(peers))

    pending = []

    def go(copy):
        copy.start()
        pending.append(copy)

    def await_into(ref, send, recv, device):
        remote(ref, ref, send, recv, device).wait_recv()

    xs = (x, xl, xr, xf)
    links = {"right": right, "left": left, "z1": along_z[1], "z2": along_z[2], "z3": along_z[3]}
    sent = {}

    def place_at(way, g, d):
        if way == "right":
            return (1 if g == 0 else 3), d
        if way == "left":
            return (2 if g == 0 else 3), d
        return g, d ^ int(way[1])

    def give(way, g, d, q):
        there, depth = place_at(way, g, d)
        number = sent.setdefault((way, g, d), [len(sent), []])
        number[1].append(q)
        piece = t_all.at[xs[g] * 4 + zs[d], pl.ds(*CUTS[q])]
        remote(piece, piece, g_send.at[number[0]], g_recv.at[there * 4 + depth, q], links[way]).start()

    def take(g, d, q):
        await_into(t_all.at[xs[g] * 4 + zs[d], pl.ds(*CUTS[q])], g_send.at[0], g_recv.at[g * 4 + d, q], right)

    def give_x(d, q):
        give("right", 0, d, q)
        give("left", 0, d, q)

    def from_sides(d, q):
        take(1, d, q)
        if q < 2:
            give("right", 1, d, q)
        take(2, d, q)
        if q >= 2:
            give("left", 2, d, q)

    every = range(4)
    for way in ("right", "left", "z1", "z2", "z3"):
        for q in every:
            give(way, 0, 0, q)

    l_f32[...] = jnp.zeros_like(l_f32)
    for part_no in range(2):
        v_cat[pl.ds(part_no * KP + K, KP - K), :] = jnp.zeros((KP - K, 1024), BF16)
    v_copy.wait()

    def split_v(i, carry):
        value = v_in[pl.ds(pl.multiple_of(i * 80, 80), 80), :]
        high = value.astype(BF16)
        low = (value - high.astype(F32)).astype(BF16)
        v_cat[pl.ds(pl.multiple_of(i * 80, 16), 80), :] = high
        v_cat[pl.ds(pl.multiple_of(KP + i * 80, 16), 80), :] = low
        return carry

    lax.fori_loop(0, K // 80, split_v, 0)
    def multiply(slots):
        many = len(slots)
        for w, slot in enumerate(slots):
            for j in range(6):
                l_f32[pl.ds(40 * w, ROWS), 128 * j : 128 * j + 128] = t_all[slot, pl.ds(ROWS * j, ROWS), :]
            for q in range(4):
                l_f32[pl.ds(40 * w + TAIL * q, TAIL), 768:800] = t_all[slot, pl.ds(ROWS * 6, TAIL), 32 * q : 32 * q + 32]
        size = 40 * many
        value = l_f32[0:size, :]
        high = value.astype(BF16)
        lhs[0:size, :] = high
        lhs[size : 2 * size, :] = (value - high.astype(F32)).astype(BF16)
        for n in range(4):
            both = jnp.dot(lhs[0 : 2 * size, :], v_cat[0:KP, 256 * n : 256 * n + 256], preferred_element_type=F32)
            rest = jnp.dot(lhs[0:size, :], v_cat[KP : 2 * KP, 256 * n : 256 * n + 256], preferred_element_type=F32)
            product = both[0:size] + (both[size : 2 * size] + rest)
            for w, slot in enumerate(slots):
                for h in range(2):
                    part[slot, :, 2 * n + h, :] = product[40 * w : 40 * w + ROWS, 128 * h : 128 * h + 128]
        for slot in slots:
            share = part.at[slot, pl.ds(OUT_ROWS * (1 - c), OUT_ROWS)]
            go(remote(share, core_in.at[slot], c_send.at[slot], c_recv.at[slot], sibling))

    for q in every:
        from_sides(0, q)
        if q >= 2:
            give("z1", 1, 0, q)
            give("z1", 2, 0, q)
    for q in (0, 1):
        take(0, 1, q)
        give_x(1, q)
    for q in every:
        take(0, 2, q)
        give_x(2, q)
    for q in every:
        from_sides(1, q)
    for q in every:
        take(0, 3, q)
        give_x(3, q)
    for q in every:
        from_sides(2, q)
    for q in (2, 3):
        take(0, 1, q)
    multiply([x * 4 + w for w in range(4)])
    for q in every:
        from_sides(3, q)
    multiply([xl * 4 + w for w in range(4)])
    multiply([xr * 4 + w for w in range(4)])
    for d in (0, 1):
        for q in every:
            take(3, d, q)
    multiply([xf * 4 + 2 * near, xf * 4 + 2 * near + 1])
    for d in (2, 3):
        for q in every:
            take(3, d, q)
    multiply([xf * 4 + 2 - 2 * near, xf * 4 + 3 - 2 * near])

    kind = (1 - zh, zh)

    def own(s):
        await_into(core_in.at[s], c_send.at[s], c_recv.at[s], sibling)
        mine = pl.ds(OUT_ROWS * c, OUT_ROWS)
        part[s, mine] = part[s, mine] + core_in[s]

    ways = ((1, plus_in, p_send, p_recv, up), (-1, minus_in, m_send, m_recv, down))
    nine = (pl.ds(0, 9), pl.ds(9, 9))

    def share_of(s, h):
        return part.at[s, pl.ds(OUT_ROWS * c + 9 * h, 9)]

    def owner(way, step, e):
        return lax.rem(y + 8 + (4 - step) * ways[way][0], 8) * 2 + kind[e]

    def hop(way, step, e, h):
        _, into, send, recv, to = ways[way]
        s = owner(way, step, e)
        if step > (0 if h == way else 1):
            await_into(into.at[step - 1, e, nine[h]], send.at[step - 1, e, h], recv.at[step - 1, e, h], to)
            mine = pl.ds(OUT_ROWS * c + 9 * h, 9)
            part[s, mine] = part[s, mine] + into[step - 1, e, nine[h]]
        go(remote(share_of(s, h), into.at[step, e, nine[h]], send.at[step, e, h], recv.at[step, e, h], to))

    for step in range(4):
        for e in range(2):
            if step == 0:
                own(owner(0, 0, e))
            for way in range(2):
                hop(way, step, e, way)
            if step < 3:
                for way in range(2):
                    own(owner(way, step + 1, e))
                    hop(way, step + 1, e, 1 - way)
    holders = (k + 2 - 4 * zh, k)
    starts = [lax.div(kk * OUT_ROWS, NO) for kk in holders]

    def indices(e, r):
        j = holders[e] * OUT_ROWS - starts[e] * NO + r
        wrap = jnp.where(j >= NO, 1, 0)
        return starts[e] + wrap, j - NO * wrap

    def mirrored(e, r):
        i, j = indices(e, r)
        other = j * NO + i
        holder = lax.div(other * 3641, 65536)
        return holder, other - holder * OUT_ROWS

    def row_copy(e, r, holder, place):
        return remote(total.at[e, r], flip.at[zh, place], r_send.at[e, r], r_recv.at[zh, place], (m, holder))

    def send_row(e, r):
        holder, place = mirrored(e, r)

        @pl.when(holder != k)
        def _():
            row_copy(e, r, holder, place).start()

        @pl.when(holder == k)
        def _():
            flip[zh, place] = total[e, r]

    for e in range(2):
        s = y * 2 + kind[e]
        own(s)
        for h in range(2):
            for _, into, send, recv, to in ways:
                await_into(into.at[3, e, nine[h]], send.at[3, e, h], recv.at[3, e, h], to)
            total[e, nine[h]] = part[s, pl.ds(OUT_ROWS * c + 9 * h, 9)] + (plus_in[3, e, nine[h]] + minus_in[3, e, nine[h]])
            if e == 0:
                go(remote(total.at[0, nine[h]], z_in.at[nine[h]], h_send.at[h], h_recv.at[h], across))

            def send_rows(r, carry, e=e):
                send_row(e, r)
                return carry

            lax.fori_loop(9 * h, 9 * h + 9, send_rows, 0)

    for copy in small:
        copy.wait()
    lane = lax.broadcasted_iota(jnp.int32, (8, 128), 1)
    sublane = lax.broadcasted_iota(jnp.int32, (8, 128), 0)
    energy = jnp.zeros((8, 128), F32)
    for q in range(8):
        energy = jnp.where(sublane == q, virt[m * 8 + q], energy)
    energy = energy + jnp.broadcast_to(virt_row[...], (8, 128))
    for copy in pending:
        copy.wait_send()

    for (way, g, d), (number, pieces_sent) in sent.items():
        first, last = min(pieces_sent), max(pieces_sent)
        start = CUTS[first][0]
        span = t_all.at[xs[g] * 4 + zs[d], pl.ds(start, sum(CUTS[last]) - start)]
        remote(span, span, g_send.at[number], g_recv.at[0, 0], links[way]).wait_send()

    def wait_row(r, carry):
        natural, _ = mirrored(1, r)
        for side in range(2):
            source = natural + 2 * (side - lax.rem(lax.div(natural, 2), 2))

            @pl.when(source != k)
            def _():
                await_into(flip.at[side, r], r_send.at[0, 0], r_recv.at[side, r], (m, source))

        return carry

    lax.fori_loop(0, OUT_ROWS, wait_row, 0)

    rows = flip[0] + flip[1]
    filled = jnp.concatenate([rows, jnp.zeros((32 - OUT_ROWS, 8, 128), F32)], axis=0)
    turned[...] = filled.reshape(256, 128).T.reshape(16, 8, 256)

    def piece_copy(d):
        to = lax.rem(m + d, 16)
        return remote(turned.at[to], pieces.at[m], a_send.at[d], a_recv.at[d], (to, k))

    def send_piece(d, carry):
        piece_copy(d).start()
        return carry

    lax.fori_loop(1, 16, send_piece, 0)
    pieces[m] = turned[m]

    def left_row(r, carry):
        for e in range(2):
            holder, place = mirrored(e, r)

            @pl.when(holder != k)
            def _():
                row_copy(e, r, holder, place).wait_send()

        return carry

    lax.fori_loop(0, OUT_ROWS, left_row, 0)
    for h in range(2):
        await_into(z_in.at[nine[h]], h_send.at[h], h_recv.at[h], across)

    def wait_piece(d, carry):
        source = lax.rem(m + 16 - d, 16)
        await_into(pieces.at[source], a_send.at[d], a_recv.at[d], (source, k))
        piece_copy(d).wait_send()
        return carry

    lax.fori_loop(1, 16, wait_piece, 0)

    low = [pltpu.roll(pieces[q, :, 0:128], 8 * q, 1) if q else pieces[q, :, 0:128] for q in range(16)]
    top = [pltpu.roll(pieces[q, :, 128:256], 8 * q, 1) if q else pieces[q, :, 128:256] for q in range(16)]
    for r in range(OUT_ROWS):
        have = low if r < 16 else top
        shift = r % 16
        mixed = have[0]
        for q in range(1, 16):
            mixed = jnp.where(lane // 8 == (shift + q) % 16, have[q], mixed)
        mirror = pltpu.roll(mixed, 128 - 8 * shift, 1) if shift else mixed
        i, j = indices(1, r)
        done[r] = (total[1, r] + z_in[r] + mirror) / (energy - (occ[i] + occ[j]))
    for q in range(8):
        out[:, 128 * q : 128 * q + 128] = done[:, q, :]


def body(amplitudes, integrals, occupied_energy, virtual_energy):
    dma = pltpu.SemaphoreType.DMA
    call = pl.pallas_call(
        kernel,
        out_shape=jax.ShapeDtypeStruct((OUT_ROWS, 1024), F32),
        in_specs=[pl.BlockSpec(memory_space=pltpu.HBM)] * 5,
        out_specs=pl.BlockSpec(memory_space=pltpu.VMEM),
        scratch_shapes=[
            pltpu.VMEM((ROWS, K), F32),
            pltpu.VMEM((K, 1024), F32),
            pltpu.SMEM((NO,), F32),
            pltpu.SMEM((AW,), F32),
            pltpu.VMEM((1, AW), F32),
            pltpu.VMEM((2 * KP, 1024), BF16),
            pltpu.VMEM((16, PACK, 128), F32),
            pltpu.VMEM((160, KP), F32),
            pltpu.VMEM((320, KP), BF16),
            pltpu.VMEM((16, ROWS, 8, 128), F32),
            pltpu.VMEM((16, OUT_ROWS, 8, 128), F32),
            pltpu.VMEM((4, 2, OUT_ROWS, 8, 128), F32),
            pltpu.VMEM((4, 2, OUT_ROWS, 8, 128), F32),
            pltpu.VMEM((OUT_ROWS, 8, 128), F32),
            pltpu.VMEM((2, OUT_ROWS, 8, 128), F32),
            pltpu.VMEM((2, OUT_ROWS, 8, 128), F32),
            pltpu.VMEM((16, 8, 256), F32),
            pltpu.VMEM((16, 8, 256), F32),
            pltpu.VMEM((OUT_ROWS, 8, 128), F32),
            dma((5,)),
            dma((21,)), dma((16, 4)),
            dma((16,)), dma((16,)),
            dma((4, 2, 2)), dma((4, 2, 2)), dma((4, 2, 2)), dma((4, 2, 2)),
            dma((2,)), dma((2,)),
            dma((2, OUT_ROWS)), dma((2, OUT_ROWS)),
            dma((16,)), dma((16,)),
        ],
        compiler_params=pltpu.CompilerParams(
            collective_id=0, has_side_effects=True, vmem_limit_bytes=48 * 1024 * 1024
        ),
    )
    return call(
        *(
            pltpu.with_memory_space_constraint(value, pltpu.HBM)
            for value in (
                amplitudes,
                integrals.T,
                occupied_energy,
                virtual_energy,
                virtual_energy.reshape(1, AW),
            )
        )
    )


def solution(mesh):
    return jax.shard_map(
        body,
        mesh=mesh,
        in_specs=(P("ab", "cd"), P("ab", "cd"), P(), P()),
        out_specs=P("cd", "ab"),
        check_vma=False,
    )
```

```python
import functools

import jax
import jax.numpy as jnp
from jax import lax
from jax.experimental import pallas as pl
from jax.experimental.pallas import tpu as pltpu
from jax.sharding import PartitionSpec as P

AW = 128
NO = 24
K = 800
KP = 896
ROWS = 36
OUT_ROWS = 18
PACK = 232
TAIL = 9
CUTS = ((0, 56), (56, 64), (120, 56), (176, 56))
MESH = pl.DeviceIdType.MESH
F32 = jnp.float32
BF16 = jnp.bfloat16


def remote(src, dst, send, recv, device):
    return pltpu.make_async_remote_copy(
        src_ref=src,
        dst_ref=dst,
        send_sem=send,
        recv_sem=recv,
        device_id=device,
        device_id_type=MESH,
    )


def kernel(
    t_hbm, v_hbm, occ_hbm, virt_hbm, row_hbm, out,
    t_in, v_in, occ, virt, virt_row, v_cat, t_all, l_f32, lhs, part, core_in, plus_in, minus_in, z_in, total, flip,
    turned, pieces, done,
    local_sem, g_send, g_recv,
    c_send, c_recv, p_send, p_recv, m_send, m_recv, h_send, h_recv, r_send, r_recv, a_send, a_recv,
):
    m, k = lax.axis_index("ab"), lax.axis_index("cd")
    x, z = lax.div(m, 4), lax.rem(m, 4)
    y, zh, c = lax.div(k, 4), lax.rem(lax.div(k, 2), 2), lax.rem(k, 2)
    xl, xr, xf = lax.rem(x + 3, 4), lax.rem(x + 1, 4), lax.rem(x + 2, 4)
    zs = (z, z + 1 - 2 * lax.rem(z, 2), lax.rem(z + 2, 4), 3 - z)
    near = lax.div(z, 2)
    left, right = (xl * 4 + z, k), (xr * 4 + z, k)
    along_z = [(x * 4 + zs[d], k) for d in range(4)]
    sibling = (m, k + 1 - 2 * c)
    up = (m, lax.rem(y + 1, 8) * 4 + lax.rem(k, 4))
    down = (m, lax.rem(y + 7, 8) * 4 + lax.rem(k, 4))
    across = (m, k + 2 - 4 * zh)

    t_copy = pltpu.make_async_copy(t_hbm, t_in, local_sem.at[0])
    t_copy.start()
    v_copy = pltpu.make_async_copy(v_hbm, v_in, local_sem.at[1])
    v_copy.start()
    small = [
        pltpu.make_async_copy(occ_hbm, occ, local_sem.at[2]),
        pltpu.make_async_copy(virt_hbm, virt, local_sem.at[3]),
        pltpu.make_async_copy(row_hbm, virt_row, local_sem.at[4]),
    ]
    for copy in small:
        copy.start()
    barrier = pltpu.get_barrier_semaphore()
    peers = (left, right, *along_z[1:], sibling, up, down, across)
    for peer in peers:
        pl.semaphore_signal(barrier, inc=1, device_id=peer, device_id_type=MESH)

    t_copy.wait()
    for j in range(6):
        t_all[m, pl.ds(ROWS * j, ROWS), :] = t_in[:, 128 * j : 128 * j + 128]
    t_all[m, pl.ds(ROWS * 6, TAIL), :] = jnp.concatenate(
        [t_in[TAIL * q : TAIL * q + TAIL, 768:800] for q in range(4)], axis=1
    )
    t_all[m, pl.ds(ROWS * 6 + TAIL, PACK - ROWS * 6 - TAIL), :] = jnp.zeros((PACK - ROWS * 6 - TAIL, 128), F32)
    pl.semaphore_wait(barrier, len(peers))

    pending = []

    def go(copy):
        copy.start()
        pending.append(copy)

    def await_into(ref, send, recv, device):
        remote(ref, ref, send, recv, device).wait_recv()

    xs = (x, xl, xr, xf)
    links = {"right": right, "left": left, "z1": along_z[1], "z2": along_z[2], "z3": along_z[3]}
    sent = {}

    def place_at(way, g, d):
        if way == "right":
            return (1 if g == 0 else 3), d
        if way == "left":
            return (2 if g == 0 else 3), d
        return g, d ^ int(way[1])

    def give(way, g, d, q):
        there, depth = place_at(way, g, d)
        number = sent.setdefault((way, g, d), [len(sent), []])
        number[1].append(q)
        piece = t_all.at[xs[g] * 4 + zs[d], pl.ds(*CUTS[q])]
        remote(piece, piece, g_send.at[number[0]], g_recv.at[there * 4 + depth, q], links[way]).start()

    def take(g, d, q):
        await_into(t_all.at[xs[g] * 4 + zs[d], pl.ds(*CUTS[q])], g_send.at[0], g_recv.at[g * 4 + d, q], right)

    def give_x(d, q):
        give("right", 0, d, q)
        give("left", 0, d, q)

    def from_sides(d, q):
        take(1, d, q)
        if q < 2:
            give("right", 1, d, q)
        take(2, d, q)
        if q >= 2:
            give("left", 2, d, q)

    every = range(4)
    for way in ("right", "left", "z1", "z2", "z3"):
        for q in every:
            give(way, 0, 0, q)

    l_f32[...] = jnp.zeros_like(l_f32)
    for part_no in range(2):
        v_cat[pl.ds(part_no * KP + K, KP - K), :] = jnp.zeros((KP - K, 1024), BF16)
    v_copy.wait()

    def split_v(i, carry):
        value = v_in[pl.ds(pl.multiple_of(i * 80, 80), 80), :]
        high = value.astype(BF16)
        low = (value - high.astype(F32)).astype(BF16)
        v_cat[pl.ds(pl.multiple_of(i * 80, 16), 80), :] = high
        v_cat[pl.ds(pl.multiple_of(KP + i * 80, 16), 80), :] = low
        return carry

    lax.fori_loop(0, K // 80, split_v, 0)
    def multiply(slots):
        many = len(slots)
        for w, slot in enumerate(slots):
            for j in range(6):
                l_f32[pl.ds(40 * w, ROWS), 128 * j : 128 * j + 128] = t_all[slot, pl.ds(ROWS * j, ROWS), :]
            for q in range(4):
                l_f32[pl.ds(40 * w + TAIL * q, TAIL), 768:800] = t_all[slot, pl.ds(ROWS * 6, TAIL), 32 * q : 32 * q + 32]
        size = 40 * many
        value = l_f32[0:size, :]
        high = value.astype(BF16)
        lhs[0:size, :] = high
        lhs[size : 2 * size, :] = (value - high.astype(F32)).astype(BF16)
        for n in range(4):
            both = jnp.dot(lhs[0 : 2 * size, :], v_cat[0:KP, 256 * n : 256 * n + 256], preferred_element_type=F32)
            rest = jnp.dot(lhs[0:size, :], v_cat[KP : 2 * KP, 256 * n : 256 * n + 256], preferred_element_type=F32)
            product = both[0:size] + (both[size : 2 * size] + rest)
            for w, slot in enumerate(slots):
                for h in range(2):
                    part[slot, :, 2 * n + h, :] = product[40 * w : 40 * w + ROWS, 128 * h : 128 * h + 128]
        for slot in slots:
            share = part.at[slot, pl.ds(OUT_ROWS * (1 - c), OUT_ROWS)]
            go(remote(share, core_in.at[slot], c_send.at[slot], c_recv.at[slot], sibling))

    def pair(g, d):
        first = xs[g] * 4 + 2 * (near if d == 0 else 1 - near)
        multiply([first, first + 1])

    for q in every:
        from_sides(0, q)
        if q >= 2:
            give("z1", 1, 0, q)
            give("z1", 2, 0, q)
    for q in (0, 1):
        take(0, 1, q)
        give_x(1, q)
    for q in every:
        take(0, 2, q)
        give_x(2, q)
    for q in (2, 3):
        take(0, 1, q)
    pair(0, 0)
    for q in every:
        from_sides(1, q)
    for q in every:
        take(0, 3, q)
        give_x(3, q)
    for q in every:
        from_sides(2, q)
    pair(0, 1)
    pair(1, 0)
    pair(2, 0)
    for q in every:
        from_sides(3, q)
    pair(1, 1)
    pair(2, 1)
    for q in every:
        take(3, 0, q)
    for q in every:
        take(3, 1, q)
    pair(3, 0)
    for q in every:
        take(3, 2, q)
    for q in every:
        take(3, 3, q)
    pair(3, 1)

    kind = (1 - zh, zh)

    def own(s):
        await_into(core_in.at[s], c_send.at[s], c_recv.at[s], sibling)
        mine = pl.ds(OUT_ROWS * c, OUT_ROWS)
        part[s, mine] = part[s, mine] + core_in[s]

    ways = ((1, plus_in, p_send, p_recv, up), (-1, minus_in, m_send, m_recv, down))
    nine = (pl.ds(0, 9), pl.ds(9, 9))

    def share_of(s, h):
        return part.at[s, pl.ds(OUT_ROWS * c + 9 * h, 9)]

    def owner(way, step, e):
        return lax.rem(y + 8 + (4 - step) * ways[way][0], 8) * 2 + kind[e]

    def hop(way, step, e, h):
        _, into, send, recv, to = ways[way]
        s = owner(way, step, e)
        if step > (0 if h == way else 1):
            await_into(into.at[step - 1, e, nine[h]], send.at[step - 1, e, h], recv.at[step - 1, e, h], to)
            mine = pl.ds(OUT_ROWS * c + 9 * h, 9)
            part[s, mine] = part[s, mine] + into[step - 1, e, nine[h]]
        go(remote(share_of(s, h), into.at[step, e, nine[h]], send.at[step, e, h], recv.at[step, e, h], to))

    for step in range(4):
        for e in range(2):
            if step == 0:
                own(owner(0, 0, e))
            for way in range(2):
                hop(way, step, e, way)
            if step < 3:
                for way in range(2):
                    own(owner(way, step + 1, e))
                    hop(way, step + 1, e, 1 - way)
    holders = (k + 2 - 4 * zh, k)
    starts = [lax.div(kk * OUT_ROWS, NO) for kk in holders]

    def indices(e, r):
        j = holders[e] * OUT_ROWS - starts[e] * NO + r
        wrap = jnp.where(j >= NO, 1, 0)
        return starts[e] + wrap, j - NO * wrap

    def mirrored(e, r):
        i, j = indices(e, r)
        other = j * NO + i
        holder = lax.div(other * 3641, 65536)
        return holder, other - holder * OUT_ROWS

    def row_copy(e, r, holder, place):
        return remote(total.at[e, r], flip.at[zh, place], r_send.at[e, r], r_recv.at[zh, place], (m, holder))

    def send_row(e, r):
        holder, place = mirrored(e, r)

        @pl.when(holder != k)
        def _():
            row_copy(e, r, holder, place).start()

        @pl.when(holder == k)
        def _():
            flip[zh, place] = total[e, r]

    for e in range(2):
        s = y * 2 + kind[e]
        own(s)
        for h in range(2):
            for _, into, send, recv, to in ways:
                await_into(into.at[3, e, nine[h]], send.at[3, e, h], recv.at[3, e, h], to)
            total[e, nine[h]] = part[s, pl.ds(OUT_ROWS * c + 9 * h, 9)] + (plus_in[3, e, nine[h]] + minus_in[3, e, nine[h]])
            if e == 0:
                go(remote(total.at[0, nine[h]], z_in.at[nine[h]], h_send.at[h], h_recv.at[h], across))

            def send_rows(r, carry, e=e):
                send_row(e, r)
                return carry

            lax.fori_loop(9 * h, 9 * h + 9, send_rows, 0)

    for copy in small:
        copy.wait()
    lane = lax.broadcasted_iota(jnp.int32, (8, 128), 1)
    sublane = lax.broadcasted_iota(jnp.int32, (8, 128), 0)
    energy = jnp.zeros((8, 128), F32)
    for q in range(8):
        energy = jnp.where(sublane == q, virt[m * 8 + q], energy)
    energy = energy + jnp.broadcast_to(virt_row[...], (8, 128))
    for copy in pending:
        copy.wait_send()

    for (way, g, d), (number, pieces_sent) in sent.items():
        first, last = min(pieces_sent), max(pieces_sent)
        start = CUTS[first][0]
        span = t_all.at[xs[g] * 4 + zs[d], pl.ds(start, sum(CUTS[last]) - start)]
        remote(span, span, g_send.at[number], g_recv.at[0, 0], links[way]).wait_send()

    def wait_row(r, carry):
        natural, _ = mirrored(1, r)
        for side in range(2):
            source = natural + 2 * (side - lax.rem(lax.div(natural, 2), 2))

            @pl.when(source != k)
            def _():
                await_into(flip.at[side, r], r_send.at[0, 0], r_recv.at[side, r], (m, source))

        return carry

    lax.fori_loop(0, OUT_ROWS, wait_row, 0)

    rows = flip[0] + flip[1]
    filled = jnp.concatenate([rows, jnp.zeros((32 - OUT_ROWS, 8, 128), F32)], axis=0)
    turned[...] = filled.reshape(256, 128).T.reshape(16, 8, 256)

    def piece_copy(d):
        to = lax.rem(m + d, 16)
        return remote(turned.at[to], pieces.at[m], a_send.at[d], a_recv.at[d], (to, k))

    def send_piece(d, carry):
        piece_copy(d).start()
        return carry

    lax.fori_loop(1, 16, send_piece, 0)
    pieces[m] = turned[m]

    def left_row(r, carry):
        for e in range(2):
            holder, place = mirrored(e, r)

            @pl.when(holder != k)
            def _():
                row_copy(e, r, holder, place).wait_send()

        return carry

    lax.fori_loop(0, OUT_ROWS, left_row, 0)
    for h in range(2):
        await_into(z_in.at[nine[h]], h_send.at[h], h_recv.at[h], across)

    def wait_piece(d, carry):
        source = lax.rem(m + 16 - d, 16)
        await_into(pieces.at[source], a_send.at[d], a_recv.at[d], (source, k))
        piece_copy(d).wait_send()
        return carry

    lax.fori_loop(1, 16, wait_piece, 0)

    low = [pltpu.roll(pieces[q, :, 0:128], 8 * q, 1) if q else pieces[q, :, 0:128] for q in range(16)]
    top = [pltpu.roll(pieces[q, :, 128:256], 8 * q, 1) if q else pieces[q, :, 128:256] for q in range(16)]
    for r in range(OUT_ROWS):
        have = low if r < 16 else top
        shift = r % 16
        mixed = have[0]
        for q in range(1, 16):
            mixed = jnp.where(lane // 8 == (shift + q) % 16, have[q], mixed)
        mirror = pltpu.roll(mixed, 128 - 8 * shift, 1) if shift else mixed
        i, j = indices(1, r)
        done[r] = (total[1, r] + z_in[r] + mirror) / (energy - (occ[i] + occ[j]))
    for q in range(8):
        out[:, 128 * q : 128 * q + 128] = done[:, q, :]


def body(amplitudes, integrals, occupied_energy, virtual_energy):
    dma = pltpu.SemaphoreType.DMA
    call = pl.pallas_call(
        kernel,
        out_shape=jax.ShapeDtypeStruct((OUT_ROWS, 1024), F32),
        in_specs=[pl.BlockSpec(memory_space=pltpu.HBM)] * 5,
        out_specs=pl.BlockSpec(memory_space=pltpu.VMEM),
        scratch_shapes=[
            pltpu.VMEM((ROWS, K), F32),
            pltpu.VMEM((K, 1024), F32),
            pltpu.SMEM((NO,), F32),
            pltpu.SMEM((AW,), F32),
            pltpu.VMEM((1, AW), F32),
            pltpu.VMEM((2 * KP, 1024), BF16),
            pltpu.VMEM((16, PACK, 128), F32),
            pltpu.VMEM((160, KP), F32),
            pltpu.VMEM((320, KP), BF16),
            pltpu.VMEM((16, ROWS, 8, 128), F32),
            pltpu.VMEM((16, OUT_ROWS, 8, 128), F32),
            pltpu.VMEM((4, 2, OUT_ROWS, 8, 128), F32),
            pltpu.VMEM((4, 2, OUT_ROWS, 8, 128), F32),
            pltpu.VMEM((OUT_ROWS, 8, 128), F32),
            pltpu.VMEM((2, OUT_ROWS, 8, 128), F32),
            pltpu.VMEM((2, OUT_ROWS, 8, 128), F32),
            pltpu.VMEM((16, 8, 256), F32),
            pltpu.VMEM((16, 8, 256), F32),
            pltpu.VMEM((OUT_ROWS, 8, 128), F32),
            dma((5,)),
            dma((21,)), dma((16, 4)),
            dma((16,)), dma((16,)),
            dma((4, 2, 2)), dma((4, 2, 2)), dma((4, 2, 2)), dma((4, 2, 2)),
            dma((2,)), dma((2,)),
            dma((2, OUT_ROWS)), dma((2, OUT_ROWS)),
            dma((16,)), dma((16,)),
        ],
        compiler_params=pltpu.CompilerParams(
            collective_id=0, has_side_effects=True, vmem_limit_bytes=48 * 1024 * 1024
        ),
    )
    return call(
        *(
            pltpu.with_memory_space_constraint(value, pltpu.HBM)
            for value in (
                amplitudes,
                integrals.T,
                occupied_energy,
                virtual_energy,
                virtual_energy.reshape(1, AW),
            )
        )
    )


def solution(mesh):
    return jax.shard_map(
        body,
        mesh=mesh,
        in_specs=(P("ab", "cd"), P("ab", "cd"), P(), P()),
        out_specs=P("cd", "ab"),
        check_vma=False,
    )
```
